32 devices in a mesh: dp: 8 (over z, core), tensor: 4 (over y, x).
Axes of the slice: x: 2, y: 2, z: 4, core: 2. Of those that a mesh axis runs over, the one named last changes fastest.
Arguments:
- hidden_in: bfloat16 [16384, 1024], P(('dp', 'tensor')), may hold values from -6 to 6
- ln1_gain: bfloat16 [1024], P(('dp', 'tensor')), may hold values from 0.25 to 1.75
- ln1_bias: bfloat16 [1024], P(('dp', 'tensor')), may hold values from -1.5 to 1.5
- qkv_weight: bfloat16 [1024, 3, 1024], P('dp', None, 'tensor'), may hold values from -0.1875 to 0.1875
- qv_bias: bfloat16 [2048], P(('dp', 'tensor')), may hold values from -1.5 to 1.5
- out_weight: bfloat16 [1024, 1024], P('dp', 'tensor'), may hold values from -0.75 to 0.75
- out_bias: bfloat16 [1024], P(('dp', 'tensor')), may hold values from -1.5 to 1.5
- ln2_gain: bfloat16 [1024], P(('dp', 'tensor')), may hold values from 0.25 to 1.75
- ln2_bias: bfloat16 [1024], P(('dp', 'tensor')), may hold values from -1.5 to 1.5
- fc_weight: bfloat16 [1024, 4096], P('dp', 'tensor'), may hold values from -0.1875 to 0.1875
- fc_bias: bfloat16 [4096], P(('dp', 'tensor')), may hold values from -1.5 to 1.5
- proj_weight: bfloat16 [1024, 4096], P('dp', 'tensor'), may hold values from -0.09375 to 0.09375
- proj_bias: bfloat16 [1024], P(('dp', 'tensor')), may hold values from -1.5 to 1.5
- segment_ids: int32 [16384], P('dp'), may hold values from 0 to 1, as said below
- out_grad: bfloat16 [16384, 1024], P(('dp', 'tensor')), may hold values from -6 to 6
Outputs:
- layer_out: bfloat16 [16384, 1024], P(('dp', 'tensor'))
- in_grad: bfloat16 [16384, 1024], P(('dp', 'tensor'))
- grad_ln1_gain: float32 [1024], P(('dp', 'tensor'))
- grad_ln1_bias: float32 [1024], P(('dp', 'tensor'))
- grad_qkv_weight: float32 [1024, 3, 1024], P('dp', None, 'tensor')
- grad_qv_bias: float32 [2048], P(('dp', 'tensor'))
- grad_out_weight: float32 [1024, 1024], P('dp', 'tensor')
- grad_out_bias: float32 [1024], P(('dp', 'tensor'))
- grad_ln2_gain: float32 [1024], P(('dp', 'tensor'))
- grad_ln2_bias: float32 [1024], P(('dp', 'tensor'))
- grad_fc_weight: float32 [1024, 4096], P('dp', 'tensor')
- grad_fc_bias: float32 [4096], P(('dp', 'tensor'))
- grad_proj_weight: float32 [1024, 4096], P('dp', 'tensor')
- grad_proj_bias: float32 [1024], P(('dp', 'tensor'))
The draws below stay inside these ranges and needn't reach their ends.
Inputs may be any that keep to these rules, and one draw needn't show every extreme that they name: `segment_ids`: each aligned block of 2048 tokens (one data group) holds whole sequences: ids start at 0 on its first token, stay equal within a sequence and rise by one at the next; each sequence has 1024 tokens or more, or the whole block where that is shorter.
All inputs are finite; a program needn't handle non-finite values.
Results may differ from the reference program's by a relative error of at most 0.02.
Values may be sent and summed in bfloat16 or wider, within the bound.
A program may use at most 384 MiB of HBM per device.

```python
import jax
import jax.numpy as jnp
from jax import lax

D = 1024
HEADS = 16
HD = 64
FF = 4096
MIN_LEN = 1024
GROUP = 2048
TOKENS = 16384
N_DP = 8


def draw_segment_ids(key, part):
    key = jax.random.fold_in(key, 7)
    least_len = min(MIN_LEN, GROUP)
    step_count = GROUP // least_len
    positions = jnp.arange(GROUP, dtype=jnp.int32)
    pick_key, groups_key = jax.random.split(key)
    forced_group = jax.random.randint(pick_key, (), 0, N_DP, dtype=jnp.int32)

    def one_group(group_key, forced):

        def pick_length(remain, step_key):
            coin_key, len_key = jax.random.split(step_key)
            upper_len = jnp.maximum(jnp.minimum(2 * least_len, remain - least_len), least_len)
            drawn_len = jax.random.randint(len_key, (), least_len, upper_len + 1, dtype=jnp.int32)
            coin_flip = jax.random.randint(coin_key, (), 0, 2, dtype=jnp.int32)
            short_len = jnp.where((coin_flip == 1) & (remain >= 2 * least_len), least_len, remain)
            length = jnp.where(remain > 2 * least_len, drawn_len, short_len).astype(jnp.int32)
            length = jnp.where(forced, jnp.minimum(least_len, remain), length).astype(jnp.int32)
            return (remain - length, (GROUP - remain + length).astype(jnp.int32))
        _, seq_ends = lax.scan(pick_length, jnp.int32(GROUP), jax.random.split(group_key, step_count))
        return jnp.sum((seq_ends[:, None] <= positions[None, :]).astype(jnp.int32), axis=0)
    group_flags = jnp.arange(N_DP, dtype=jnp.int32) == forced_group
    return jax.vmap(one_group)(jax.random.split(groups_key, N_DP), group_flags).reshape(TOKENS).astype(jnp.int32)


def steps_of(rng, shape, cuts, least, high):
    level = 1.0
    for dim, blocks in cuts:
        steps = jax.random.uniform(jax.random.fold_in(jax.random.fold_in(rng, 6), dim), (blocks,), jnp.float32, least / len(cuts), high / len(cuts))
        level = level * jnp.repeat(jnp.exp(steps), shape[dim] // blocks).reshape((-1,) + (1,) * (len(shape) - 1 - dim))
    return level


def bell_draw(own_key, extent, scale, most, pieces=(), kind=jnp.bfloat16):
    array = scale * jax.random.normal(own_key, extent, jnp.float32)
    if pieces:
        array = array * steps_of(own_key, extent, pieces, -0.22, 0.18)
    return jnp.clip(array, -most, most).astype(kind)


def setup_inputs(seed: int = 0) -> dict:
    key_list = jax.random.split(jax.random.key(seed), 16)
    return {
        "hidden_in": bell_draw(key_list[0], (TOKENS, D), 1.0, 6.0, ((0, 32),)),
        "ln1_gain": jnp.clip(1.0 + 0.15 * jax.random.normal(key_list[1], (D,), jnp.float32), 0.25, 1.75).astype(jnp.bfloat16),
        "ln1_bias": bell_draw(key_list[2], (D,), 0.3, 1.5, ((0, 32),)),
        "qkv_weight": bell_draw(key_list[3], (D, 3, D), D ** -0.5, 0.1875, ((0, 8), (2, 4))),
        "qv_bias": bell_draw(key_list[4], (2 * D,), 0.3, 1.5, ((0, 32),)),
        "out_weight": bell_draw(key_list[5], (D, D), (D // 16) ** -0.5, 0.75, ((0, 8), (1, 4))),
        "out_bias": bell_draw(key_list[6], (D,), 0.3, 1.5, ((0, 32),)),
        "ln2_gain": jnp.clip(1.0 + 0.15 * jax.random.normal(key_list[7], (D,), jnp.float32), 0.25, 1.75).astype(jnp.bfloat16),
        "ln2_bias": bell_draw(key_list[8], (D,), 0.3, 1.5, ((0, 32),)),
        "fc_weight": bell_draw(key_list[9], (D, FF), D ** -0.5, 0.1875, ((0, 8), (1, 4))),
        "fc_bias": bell_draw(key_list[10], (FF,), 0.3, 1.5, ((0, 32),)),
        "proj_weight": bell_draw(key_list[11], (D, FF), FF ** -0.5, 0.09375, ((0, 8), (1, 4))),
        "proj_bias": bell_draw(key_list[12], (D,), 0.3, 1.5, ((0, 32),)),
        "segment_ids": draw_segment_ids(jax.random.fold_in(key_list[15], 71), 0),
        "out_grad": bell_draw(key_list[14], (TOKENS, D), 1.0, 6.0, ((0, 32),)),
    }


NEG_FILL = -1e+30
EPSILON = 1e-05
PRECISE = lax.Precision.HIGHEST

@jax.custom_vjp
def low(v):
    return lax.optimization_barrier(v.astype(jnp.bfloat16)).astype(jnp.float32)

@jax.custom_vjp
def low_back(v):
    return v

def low_keep(v):
    return (low(v), None)

def low_pass(kept, grad):
    return (grad,)

def back_keep(v):
    return (v, None)

def back_low(kept, grad):
    return (low(grad),)
low.defvjp(low_keep, low_pass)
low_back.defvjp(back_keep, back_low)

def layer_norm(values, gain_vec, shift_vec):
    center = values - lax.optimization_barrier(jnp.mean(values, axis=-1, keepdims=True))
    spread = lax.optimization_barrier(jnp.mean(center * center, axis=-1, keepdims=True))
    return center * lax.rsqrt(spread + EPSILON) * gain_vec + shift_vec

def gelu_tanh(values):
    return jax.nn.gelu(values, approximate=True)

def attention(queries, keys, vals, segments):
    group_rows = queries.shape[0]
    block_rows = min(group_rows, 512)
    slopes = 2.0 ** (-8.0 * jnp.arange(1, HEADS + 1, dtype=jnp.float32) / HEADS)
    positions = jnp.arange(group_rows, dtype=jnp.int32)

    def one_block(start_row):
        query_rows = lax.dynamic_slice_in_dim(queries, start_row, block_rows, 0)
        query_seg = lax.dynamic_slice_in_dim(segments, start_row, block_rows, 0)
        raw_scores = jnp.einsum('qhe,khe->hqk', query_rows, keys, precision=PRECISE) * HD ** (-0.5)
        query_pos = start_row + jnp.arange(block_rows, dtype=jnp.int32)
        distance = (positions[None, :] - query_pos[:, None]).astype(jnp.float32)
        raw_scores = raw_scores + slopes[:, None, None] * distance[None]
        scores = low_back(raw_scores)
        allowed = (query_seg[:, None] == segments[None, :]) & (positions[None, :] <= query_pos[:, None])
        masked = jnp.where(allowed[None], scores, NEG_FILL)
        row_max = lax.optimization_barrier(jnp.max(masked, axis=-1, keepdims=True))
        exponent = jnp.exp(masked - row_max)
        probs = low(exponent / lax.optimization_barrier(jnp.sum(exponent, axis=-1, keepdims=True)))
        return jnp.einsum('hqk,khe->qhe', probs, vals, precision=PRECISE)
    starts = jnp.arange(0, group_rows, block_rows, dtype=jnp.int32)
    blocks = lax.map(jax.checkpoint(one_block), starts)
    return blocks.reshape(group_rows, HEADS * HD)

def group_layer(params, source, segments):
    gain_one, shift_one, qkv_w, qv_b, out_w, out_b, gain_two, shift_two, fc_w, fc_b, proj_w, proj_b = params
    normed_one = low(layer_norm(source, gain_one, shift_one))
    mixed = jnp.einsum('td,dcn->tcn', normed_one, qkv_w, precision=PRECISE)
    queries = low(low_back(mixed[:, 0] + qv_b[:D])).reshape(-1, HEADS, HD)
    keys = low(low_back(mixed[:, 1])).reshape(-1, HEADS, HD)
    vals = low(low_back(mixed[:, 2] + qv_b[D:])).reshape(-1, HEADS, HD)
    context = low(low_back(attention(queries, keys, vals, segments)))
    branch_one = low_back(jnp.dot(context, out_w.T, precision=PRECISE) + out_b)
    middle = source + branch_one
    normed_two = low(layer_norm(middle, gain_two, shift_two))
    pre_act = low_back(jnp.dot(normed_two, fc_w, precision=PRECISE) + fc_b)
    hidden_act = low(gelu_tanh(pre_act))
    branch_two = low_back(jnp.dot(hidden_act, proj_w.T, precision=PRECISE) + proj_b)
    return middle + branch_two

def reference(hidden_in, ln1_gain, ln1_bias, qkv_weight, qv_bias, out_weight, out_bias, ln2_gain, ln2_bias, fc_weight, fc_bias, proj_weight, proj_bias, segment_ids, out_grad):
    params = (ln1_gain.astype(jnp.float32), ln1_bias.astype(jnp.float32), qkv_weight.astype(jnp.float32), qv_bias.astype(jnp.float32), out_weight.astype(jnp.float32), out_bias.astype(jnp.float32), ln2_gain.astype(jnp.float32), ln2_bias.astype(jnp.float32), fc_weight.astype(jnp.float32), fc_bias.astype(jnp.float32), proj_weight.astype(jnp.float32), proj_bias.astype(jnp.float32))
    source = hidden_in.astype(jnp.float32).reshape(N_DP, GROUP, D)
    segments = segment_ids.reshape(N_DP, GROUP)

    def forward(weights, inputs):

        def group_step(carried, group_item):
            return (carried, jax.checkpoint(group_layer)(weights, group_item[0], group_item[1]))
        _, outputs = lax.scan(group_step, 0, (inputs, segments))
        return outputs
    result, pullback = jax.vjp(forward, params, source)
    gradients, grad_source = pullback(out_grad.astype(jnp.float32).reshape(N_DP, GROUP, D))
    g_gain_one, g_shift_one, g_qkv, g_qv, g_out, g_out_b, g_gain_two, g_shift_two, g_fc, g_fc_b, g_proj, g_proj_b = gradients
    return (result.reshape(TOKENS, D).astype(jnp.bfloat16), grad_source.reshape(TOKENS, D).astype(jnp.bfloat16), g_gain_one, g_shift_one, g_qkv, g_qv, g_out, g_out_b, g_gain_two, g_shift_two, g_fc, g_fc_b, g_proj, g_proj_b)
```

```python
import functools

import jax
import jax.numpy as jnp
from jax import lax
from jax.experimental import pallas as pl
from jax.experimental.pallas import tpu as pltpu
from jax.sharding import PartitionSpec as P

HEADS = 16
HD = 64


NEG_FILL = -1e30
EPSILON = 1e-05


def layer_norm(values, gain_vec, shift_vec):
    center = values - jnp.mean(values, axis=-1, keepdims=True)
    spread = jnp.mean(center * center, axis=-1, keepdims=True)
    return center * lax.rsqrt(spread + EPSILON) * gain_vec + shift_vec


def gelu_tanh(values):
    return jax.nn.gelu(values, approximate=True)


def contract_rows(left, right):
    return lax.dot_general(
        left, right, (((0,), (0,)), ((), ())), preferred_element_type=jnp.float32
    )


def contract_cols(left, right):
    return lax.dot_general(
        left, right, (((1,), (1,)), ((), ())), preferred_element_type=jnp.float32
    )


LOG2E = 1.4426950408889634
BLOCK = 512


def matmul(left, right):
    return jnp.dot(left, right, preferred_element_type=jnp.float32)


def mask_block(seg_col, seg_row, key_start, query_start, block):
    shape = (block, block)
    key_pos = key_start + lax.broadcasted_iota(jnp.int32, shape, 0)
    query_pos = query_start + lax.broadcasted_iota(jnp.int32, shape, 1)
    allowed = (seg_col == seg_row) & (key_pos <= query_pos)
    return jnp.where(allowed, 0.0, NEG_FILL)


def attend_kernel(
    heads, block, slope_ref, qt_ref, k_ref, vt_ref, segr_ref, segc_ref, ot_ref, lse_ref, kh, mask
):
    rows = k_ref.shape[0]
    for h in range(heads):
        kh[h] = k_ref[:, h * HD : (h + 1) * HD]
    scale = LOG2E * HD ** (-0.5)

    def query_loop(i, carry_none):
        q0 = pl.multiple_of(i * block, block)
        seg_row = segr_ref[:, pl.ds(q0, block)]

        def key_loop(j, state):
            k0 = pl.multiple_of(j * block, block)
            mask[...] = mask_block(segc_ref[pl.ds(k0, block), :], seg_row, k0, q0, block)
            pos = (k0 + lax.broadcasted_iota(jnp.int32, (block, 1), 0)).astype(jnp.float32)
            new_state = []
            for h in range(heads):
                top, total, acc = state[3 * h : 3 * h + 3]
                hs = slice(h * HD, (h + 1) * HD)
                raw = matmul(kh[h, pl.ds(k0, block), :], qt_ref[hs, pl.ds(q0, block)])
                score = raw * scale + (slope_ref[h] * pos + mask[...])
                new_top = jnp.maximum(top, jnp.max(score, axis=0, keepdims=True))
                prob = jnp.exp2(score - new_top)
                shrink = jnp.exp2(top - new_top)
                total = total * shrink + jnp.sum(prob, axis=0, keepdims=True)
                acc = acc * shrink + matmul(
                    vt_ref[hs, pl.ds(k0, block)], prob.astype(jnp.bfloat16)
                )
                new_state += [new_top, total, acc]
            return tuple(new_state)

        state = []
        for h in range(heads):
            state += [
                jnp.full((1, block), NEG_FILL, jnp.float32),
                jnp.zeros((1, block), jnp.float32),
                jnp.zeros((HD, block), jnp.float32),
            ]
        state = lax.fori_loop(0, i + 1, key_loop, tuple(state))
        for h in range(heads):
            top, total, acc = state[3 * h : 3 * h + 3]
            ot_ref[h * HD : (h + 1) * HD, pl.ds(q0, block)] = acc / total
            lse_ref[h, :, pl.ds(q0, block)] = top + jnp.log2(total)
        return carry_none

    lax.fori_loop(0, rows // block, query_loop, 0)


def attend_back_kernel(
    heads,
    block,
    slope_ref,
    q_ref,
    qt_ref,
    k_ref,
    kt_ref,
    v_ref,
    do_ref,
    dot_ref,
    ot_ref,
    lse_ref,
    segr_ref,
    segc_ref,
    dqt_ref,
    dk_ref,
    dv_ref,
    qh,
    kh,
    vh,
    doh,
    delta,
    dqt,
    mask,
):
    rows = k_ref.shape[0]
    for h in range(heads):
        hs = slice(h * HD, (h + 1) * HD)
        qh[h] = q_ref[:, hs]
        kh[h] = k_ref[:, hs]
        vh[h] = v_ref[:, hs]
        doh[h] = do_ref[:, hs]
        delta[h] = jnp.sum(dot_ref[hs, :].astype(jnp.float32) * ot_ref[hs, :], axis=0, keepdims=True)
    dqt[...] = jnp.zeros_like(dqt)
    scale = LOG2E * HD ** (-0.5)
    score_scale = HD ** (-0.5)
    count = rows // block

    def key_loop(j, carry_none):
        k0 = pl.multiple_of(j * block, block)
        pos = (k0 + lax.broadcasted_iota(jnp.int32, (block, 1), 0)).astype(jnp.float32)
        seg_col = segc_ref[pl.ds(k0, block), :]

        def query_loop(i, state):
            q0 = pl.multiple_of(i * block, block)
            mask[...] = mask_block(seg_col, segr_ref[:, pl.ds(q0, block)], k0, q0, block)
            new_state = []
            for h in range(heads):
                grad_k, grad_v = state[2 * h : 2 * h + 2]
                hs = slice(h * HD, (h + 1) * HD)
                raw = matmul(kh[h, pl.ds(k0, block), :], qt_ref[hs, pl.ds(q0, block)])
                score = raw * scale + (slope_ref[h] * pos + mask[...])
                prob = jnp.exp2(score - lse_ref[h, :, pl.ds(q0, block)])
                grad_p = matmul(vh[h, pl.ds(k0, block), :], dot_ref[hs, pl.ds(q0, block)])
                grad_s = (prob * (grad_p - delta[h, :, pl.ds(q0, block)])).astype(jnp.bfloat16)
                grad_v = grad_v + matmul(prob.astype(jnp.bfloat16), doh[h, pl.ds(q0, block), :])
                grad_k = grad_k + matmul(grad_s, qh[h, pl.ds(q0, block), :])
                dqt[hs, pl.ds(q0, block)] += matmul(kt_ref[hs, pl.ds(k0, block)], grad_s)
                new_state += [grad_k, grad_v]
            return tuple(new_state)

        zero = jnp.zeros((block, HD), jnp.float32)
        state = lax.fori_loop(j, count, query_loop, (zero,) * (2 * heads))
        for h in range(heads):
            hs = slice(h * HD, (h + 1) * HD)
            dk_ref[pl.ds(k0, block), hs] = (state[2 * h] * score_scale).astype(jnp.bfloat16)
            dv_ref[pl.ds(k0, block), hs] = state[2 * h + 1].astype(jnp.bfloat16)
        return carry_none

    lax.fori_loop(0, count, key_loop, 0)
    dqt_ref[...] = (dqt[...] * score_scale).astype(jnp.bfloat16)


def vmem_specs(count):
    return [pl.BlockSpec(memory_space=pltpu.SMEM)] + [
        pl.BlockSpec(memory_space=pltpu.VMEM) for _ in range(count)
    ]


def attend(queries_t, key_all, values_t, segments, slopes):
    rows, cols = key_all.shape
    heads = cols // HD
    block = min(BLOCK, rows)
    vm = pl.BlockSpec(memory_space=pltpu.VMEM)
    return pl.pallas_call(
        functools.partial(attend_kernel, heads, block),
        out_shape=(
            jax.ShapeDtypeStruct((cols, rows), jnp.float32),
            jax.ShapeDtypeStruct((heads, 1, rows), jnp.float32),
        ),
        in_specs=vmem_specs(5),
        out_specs=(vm, vm),
        scratch_shapes=[
            pltpu.VMEM((heads, rows, HD), jnp.bfloat16),
            pltpu.VMEM((block, block), jnp.float32),
        ],
        compiler_params=pltpu.CompilerParams(vmem_limit_bytes=48 * 2**20),
        cost_estimate=pl.CostEstimate(
            flops=40_000_000_000, bytes_accessed=8_000_000, transcendentals=0
        ),
    )(slopes * LOG2E, queries_t, key_all, values_t, segments[None, :], segments[:, None])


def attend_back(queries, queries_t, keys, values, segments, slopes, attended_t, log_sums, grad_out):
    rows, cols = keys.shape
    heads = cols // HD
    block = min(BLOCK, rows)
    vm = pl.BlockSpec(memory_space=pltpu.VMEM)
    per_head = pltpu.VMEM((heads, rows, HD), jnp.bfloat16)
    return pl.pallas_call(
        functools.partial(attend_back_kernel, heads, block),
        out_shape=(
            jax.ShapeDtypeStruct((cols, rows), jnp.bfloat16),
            jax.ShapeDtypeStruct((rows, cols), jnp.bfloat16),
            jax.ShapeDtypeStruct((rows, cols), jnp.bfloat16),
        ),
        in_specs=vmem_specs(11),
        out_specs=(vm, vm, vm),
        scratch_shapes=[
            per_head,
            per_head,
            per_head,
            per_head,
            pltpu.VMEM((heads, 1, rows), jnp.float32),
            pltpu.VMEM((cols, rows), jnp.float32),
            pltpu.VMEM((block, block), jnp.float32),
        ],
        compiler_params=pltpu.CompilerParams(vmem_limit_bytes=48 * 2**20),
        cost_estimate=pl.CostEstimate(
            flops=80_000_000_000, bytes_accessed=16_000_000, transcendentals=0
        ),
    )(
        slopes * LOG2E,
        queries,
        queries_t,
        keys,
        keys.T,
        values,
        grad_out,
        grad_out.T,
        attended_t,
        log_sums,
        segments[None, :],
        segments[:, None],
    )


def pad_lanes(values):
    return jnp.pad(values, ((0, 0), (0, -values.shape[1] % 128)))


def body(
    hidden_in,
    ln1_gain,
    ln1_bias,
    qkv_weight,
    qv_bias,
    out_weight,
    out_bias,
    ln2_gain,
    ln2_bias,
    fc_weight,
    fc_bias,
    proj_weight,
    proj_bias,
    segment_ids,
    out_grad,
):
    width = hidden_in.shape[1]
    shard_pos = lax.axis_index("tensor")
    small = (ln1_gain, ln1_bias, qv_bias, out_bias, ln2_gain, ln2_bias, fc_bias, proj_bias)
    packed = lax.all_gather(
        pad_lanes(jnp.concatenate(small)[None, :]), ("dp", "tensor"), axis=0, tiled=True
    ).astype(jnp.float32)
    device_count = packed.shape[0]
    vectors = []
    place = 0
    for vector in small:
        size = vector.shape[0]
        vectors.append(packed[:, place : place + size].reshape(device_count * size))
        place += size
    gain_one, shift_one, qv_full, out_shift, gain_two, shift_two, fc_full, proj_shift = vectors
    qkv_local, out_local, fc_local, proj_local = (
        lax.all_gather(qkv_weight, "dp", axis=0, tiled=True),
        lax.all_gather(out_weight, "dp", axis=0, tiled=True),
        lax.all_gather(fc_weight, "dp", axis=0, tiled=True),
        lax.all_gather(proj_weight, "dp", axis=0, tiled=True),
    )
    head_cols = qkv_local.shape[2]
    heads_here = head_cols // HD
    ff_cols = fc_local.shape[1]
    ff_total = fc_full.shape[0]
    slopes_all = 2.0 ** (-8.0 * jnp.arange(1, HEADS + 1, dtype=jnp.float32) / HEADS)
    slopes = lax.dynamic_slice_in_dim(slopes_all, shard_pos * heads_here, heads_here)
    q_shift = lax.dynamic_slice_in_dim(qv_full, shard_pos * head_cols, head_cols)
    v_shift = lax.dynamic_slice_in_dim(qv_full, width + shard_pos * head_cols, head_cols)
    source = hidden_in.astype(jnp.float32)
    normed_one = layer_norm(source, gain_one, shift_one)
    group_one = lax.all_gather(normed_one.astype(jnp.bfloat16), "tensor", axis=0, tiled=True)
    group_rows = group_one.shape[0]
    mixed = jnp.einsum("td,dcn->tcn", group_one, qkv_local, preferred_element_type=jnp.float32)
    queries = (mixed[:, 0] + q_shift).astype(jnp.bfloat16)
    keys_here = mixed[:, 1].astype(jnp.bfloat16)
    values_here = (mixed[:, 2] + v_shift).astype(jnp.bfloat16)
    queries_t = queries.T
    attended_t, log_sums = attend(queries_t, keys_here, values_here.T, segment_ids, slopes)
    context = attended_t.astype(jnp.bfloat16).T
    branch_one = lax.psum_scatter(
        contract_cols(context, out_local).astype(jnp.bfloat16),
        "tensor",
        scatter_dimension=0,
        tiled=True,
    ).astype(jnp.float32)
    middle = source + branch_one + out_shift
    normed_two = layer_norm(middle, gain_two, shift_two)
    low_two = normed_two.astype(jnp.bfloat16)
    group_two = lax.all_gather(low_two, "tensor", axis=0, tiled=True)
    fc_shift = lax.dynamic_slice_in_dim(fc_full, shard_pos * ff_cols, ff_cols)
    pre_act = jnp.dot(group_two, fc_local, preferred_element_type=jnp.float32) + fc_shift
    hidden_act = gelu_tanh(pre_act).astype(jnp.bfloat16)
    branch_two = (
        lax.psum_scatter(
            contract_cols(hidden_act, proj_local).astype(jnp.bfloat16),
            "tensor",
            scatter_dimension=0,
            tiled=True,
        ).astype(jnp.float32)
        + proj_shift
    )
    result = middle + branch_two
    group_top = lax.all_gather(out_grad, "tensor", axis=0, tiled=True)
    grad_hidden = jnp.dot(group_top, proj_local, preferred_element_type=jnp.float32)
    grad_proj_local = contract_rows(group_top, hidden_act)
    _, gelu_back = jax.vjp(gelu_tanh, pre_act)
    low_pre = gelu_back(grad_hidden)[0].astype(jnp.bfloat16)
    grad_fc_vec = lax.dynamic_update_slice_in_dim(
        jnp.zeros((ff_total,), jnp.float32),
        jnp.sum(low_pre.astype(jnp.float32), axis=0),
        shard_pos * ff_cols,
        0,
    )
    grad_fc_local = contract_rows(group_two, low_pre)
    grad_normed_two = lax.psum_scatter(
        contract_cols(low_pre, fc_local).astype(jnp.bfloat16),
        "tensor",
        scatter_dimension=0,
        tiled=True,
    ).astype(jnp.float32)
    grad_top = out_grad.astype(jnp.float32)
    grad_proj_vec = jnp.sum(grad_top, axis=0)
    _, norm_two_back = jax.vjp(layer_norm, middle, gain_two, shift_two)
    grad_middle_norm, grad_gain_two, grad_shift_two = norm_two_back(grad_normed_two)
    grad_middle = grad_top + grad_middle_norm
    low_mid = grad_middle.astype(jnp.bfloat16)
    grad_out_vec = jnp.sum(low_mid.astype(jnp.float32), axis=0)
    group_mid = lax.all_gather(low_mid, "tensor", axis=0, tiled=True)
    grad_context = jnp.dot(group_mid, out_local, preferred_element_type=jnp.float32)
    grad_out_local = contract_rows(group_mid, context)
    low_context = grad_context.astype(jnp.bfloat16)
    grad_query_t, grad_key, grad_value = attend_back(
        queries,
        queries_t,
        keys_here,
        values_here,
        segment_ids,
        slopes,
        attended_t,
        log_sums,
        low_context,
    )
    stacked = jnp.stack([grad_query_t.T, grad_key, grad_value], axis=1)
    grad_qkv_local = jnp.einsum(
        "td,tcn->dcn", group_one, stacked, preferred_element_type=jnp.float32
    )
    column_sums = jnp.sum(stacked.astype(jnp.float32), axis=0)
    grad_qv_vec = jnp.zeros((2 * width,), jnp.float32)
    grad_qv_vec = lax.dynamic_update_slice_in_dim(
        grad_qv_vec, column_sums[0], shard_pos * head_cols, 0
    )
    grad_qv_vec = lax.dynamic_update_slice_in_dim(
        grad_qv_vec, column_sums[2], width + shard_pos * head_cols, 0
    )
    grad_normed_one = lax.psum_scatter(
        jnp.einsum("tcn,dcn->td", stacked, qkv_local, preferred_element_type=jnp.float32).astype(
            jnp.bfloat16
        ),
        "tensor",
        scatter_dimension=0,
        tiled=True,
    ).astype(jnp.float32)
    _, norm_one_back = jax.vjp(layer_norm, source, gain_one, shift_one)
    grad_source_norm, grad_gain_one, grad_shift_one = norm_one_back(grad_normed_one)
    grad_input = grad_middle + grad_source_norm
    grad_qkv, grad_out_w, grad_fc_w, grad_proj_w = (
        lax.psum_scatter(
            grad_qkv_local.astype(jnp.bfloat16), "dp", scatter_dimension=0, tiled=True
        ).astype(jnp.float32),
        lax.psum_scatter(
            grad_out_local.astype(jnp.bfloat16), "dp", scatter_dimension=0, tiled=True
        ).astype(jnp.float32),
        lax.psum_scatter(
            grad_fc_local.astype(jnp.bfloat16), "dp", scatter_dimension=0, tiled=True
        ).astype(jnp.float32),
        lax.psum_scatter(
            grad_proj_local.astype(jnp.bfloat16), "dp", scatter_dimension=0, tiled=True
        ).astype(jnp.float32),
    )
    grads = (
        grad_gain_one,
        grad_shift_one,
        grad_qv_vec,
        grad_out_vec,
        grad_gain_two,
        grad_shift_two,
        grad_fc_vec,
        grad_proj_vec,
    )
    summed = lax.psum_scatter(
        pad_lanes(jnp.concatenate([vec.reshape(device_count, -1) for vec in grads], axis=1)),
        ("dp", "tensor"),
        scatter_dimension=0,
        tiled=True,
    ).reshape(-1)
    own = []
    place = 0
    for vector in small:
        size = vector.shape[0]
        own.append(summed[place : place + size])
        place += size
    g_gain_one, g_shift_one, g_qv, g_out_b, g_gain_two, g_shift_two, g_fc_b, g_proj_b = own
    return (
        result.astype(jnp.bfloat16),
        grad_input.astype(jnp.bfloat16),
        g_gain_one,
        g_shift_one,
        grad_qkv,
        g_qv,
        grad_out_w,
        g_out_b,
        g_gain_two,
        g_shift_two,
        grad_fc_w,
        g_fc_b,
        grad_proj_w,
        g_proj_b,
    )


def solution(mesh):
    in_specs = (
        P(("dp", "tensor"), None),
        P(("dp", "tensor")),
        P(("dp", "tensor")),
        P("dp", None, "tensor"),
        P(("dp", "tensor")),
        P("dp", "tensor"),
        P(("dp", "tensor")),
        P(("dp", "tensor")),
        P(("dp", "tensor")),
        P("dp", "tensor"),
        P(("dp", "tensor")),
        P("dp", "tensor"),
        P(("dp", "tensor")),
        P("dp"),
        P(("dp", "tensor"), None),
    )
    out_specs = (
        P(("dp", "tensor"), None),
        P(("dp", "tensor"), None),
        P(("dp", "tensor")),
        P(("dp", "tensor")),
        P("dp", None, "tensor"),
        P(("dp", "tensor")),
        P("dp", "tensor"),
        P(("dp", "tensor")),
        P(("dp", "tensor")),
        P(("dp", "tensor")),
        P("dp", "tensor"),
        P(("dp", "tensor")),
        P("dp", "tensor"),
        P(("dp", "tensor")),
    )
    return jax.shard_map(body, mesh=mesh, in_specs=in_specs, out_specs=out_specs, check_vma=False)
```

```python
import functools

import jax
import jax.numpy as jnp
from jax import lax
from jax.experimental import pallas as pl
from jax.experimental.pallas import tpu as pltpu
from jax.sharding import PartitionSpec as P

HEADS = 16
HD = 64


NEG_FILL = -1e30
EPSILON = 1e-05


def layer_norm(values, gain_vec, shift_vec):
    center = values - jnp.mean(values, axis=-1, keepdims=True)
    spread = jnp.mean(center * center, axis=-1, keepdims=True)
    return center * lax.rsqrt(spread + EPSILON) * gain_vec + shift_vec


def gelu_tanh(values):
    return jax.nn.gelu(values, approximate=True)


def contract_rows(left, right):
    return lax.dot_general(
        left, right, (((0,), (0,)), ((), ())), preferred_element_type=jnp.float32
    )


def contract_cols(left, right):
    return lax.dot_general(
        left, right, (((1,), (1,)), ((), ())), preferred_element_type=jnp.float32
    )


LOG2E = 1.4426950408889634
BLOCK = 512


def matmul(left, right):
    return jnp.dot(left, right, preferred_element_type=jnp.float32)


def mask_block(seg_col, seg_row, key_start, query_start, block):
    shape = (block, block)
    key_pos = key_start + lax.broadcasted_iota(jnp.int32, shape, 0)
    query_pos = query_start + lax.broadcasted_iota(jnp.int32, shape, 1)
    allowed = (seg_col == seg_row) & (key_pos <= query_pos)
    return jnp.where(allowed, 0.0, NEG_FILL)


def attend_kernel(
    heads, block, slope_ref, qt_ref, k_ref, vt_ref, segr_ref, segc_ref, ot_ref, lse_ref, kh, mask
):
    rows = k_ref.shape[0]
    for h in range(heads):
        kh[h] = k_ref[:, h * HD : (h + 1) * HD]
    scale = LOG2E * HD ** (-0.5)

    def query_loop(i, carry_none):
        q0 = pl.multiple_of(i * block, block)
        seg_row = segr_ref[:, pl.ds(q0, block)]

        def key_loop(j, state):
            k0 = pl.multiple_of(j * block, block)
            mask[...] = mask_block(segc_ref[pl.ds(k0, block), :], seg_row, k0, q0, block)
            pos = (k0 + lax.broadcasted_iota(jnp.int32, (block, 1), 0)).astype(jnp.float32)
            new_state = []
            for h in range(heads):
                top, total, acc = state[3 * h : 3 * h + 3]
                hs = slice(h * HD, (h + 1) * HD)
                raw = matmul(kh[h, pl.ds(k0, block), :], qt_ref[hs, pl.ds(q0, block)])
                score = raw * scale + (slope_ref[h] * pos + mask[...])
                new_top = jnp.maximum(top, jnp.max(score, axis=0, keepdims=True))
                prob = jnp.exp2(score - new_top)
                shrink = jnp.exp2(top - new_top)
                total = total * shrink + jnp.sum(prob, axis=0, keepdims=True)
                acc = acc * shrink + matmul(
                    vt_ref[hs, pl.ds(k0, block)], prob.astype(jnp.bfloat16)
                )
                new_state += [new_top, total, acc]
            return tuple(new_state)

        state = []
        for h in range(heads):
            state += [
                jnp.full((1, block), NEG_FILL, jnp.float32),
                jnp.zeros((1, block), jnp.float32),
                jnp.zeros((HD, block), jnp.float32),
            ]
        state = lax.fori_loop(0, i + 1, key_loop, tuple(state))
        for h in range(heads):
            top, total, acc = state[3 * h : 3 * h + 3]
            ot_ref[h * HD : (h + 1) * HD, pl.ds(q0, block)] = acc / total
            lse_ref[h, :, pl.ds(q0, block)] = top + jnp.log2(total)
        return carry_none

    lax.fori_loop(0, rows // block, query_loop, 0)


def attend_back_kernel(
    heads,
    block,
    slope_ref,
    q_ref,
    qt_ref,
    k_ref,
    kt_ref,
    v_ref,
    do_ref,
    dot_ref,
    ot_ref,
    lse_ref,
    segr_ref,
    segc_ref,
    dqt_ref,
    dk_ref,
    dv_ref,
    qh,
    kh,
    vh,
    doh,
    delta,
    dqt,
    mask,
):
    rows = k_ref.shape[0]
    for h in range(heads):
        hs = slice(h * HD, (h + 1) * HD)
        qh[h] = q_ref[:, hs]
        kh[h] = k_ref[:, hs]
        vh[h] = v_ref[:, hs]
        doh[h] = do_ref[:, hs]
        delta[h] = jnp.sum(dot_ref[hs, :].astype(jnp.float32) * ot_ref[hs, :], axis=0, keepdims=True)
    dqt[...] = jnp.zeros_like(dqt)
    scale = LOG2E * HD ** (-0.5)
    score_scale = HD ** (-0.5)
    count = rows // block

    def key_loop(j, carry_none):
        k0 = pl.multiple_of(j * block, block)
        pos = (k0 + lax.broadcasted_iota(jnp.int32, (block, 1), 0)).astype(jnp.float32)
        seg_col = segc_ref[pl.ds(k0, block), :]

        def query_loop(i, state):
            q0 = pl.multiple_of(i * block, block)
            mask[...] = mask_block(seg_col, segr_ref[:, pl.ds(q0, block)], k0, q0, block)
            new_state = []
            for h in range(heads):
                grad_k, grad_v = state[2 * h : 2 * h + 2]
                hs = slice(h * HD, (h + 1) * HD)
                raw = matmul(kh[h, pl.ds(k0, block), :], qt_ref[hs, pl.ds(q0, block)])
                score = raw * scale + (slope_ref[h] * pos + mask[...])
                prob = jnp.exp2(score - lse_ref[h, :, pl.ds(q0, block)])
                grad_p = matmul(vh[h, pl.ds(k0, block), :], dot_ref[hs, pl.ds(q0, block)])
                grad_s = (prob * (grad_p - delta[h, :, pl.ds(q0, block)])).astype(jnp.bfloat16)
                grad_v = grad_v + matmul(prob.astype(jnp.bfloat16), doh[h, pl.ds(q0, block), :])
                grad_k = grad_k + matmul(grad_s, qh[h, pl.ds(q0, block), :])
                dqt[hs, pl.ds(q0, block)] += matmul(kt_ref[hs, pl.ds(k0, block)], grad_s)
                new_state += [grad_k, grad_v]
            return tuple(new_state)

        zero = jnp.zeros((block, HD), jnp.float32)
        state = lax.fori_loop(j, count, query_loop, (zero,) * (2 * heads))
        for h in range(heads):
            hs = slice(h * HD, (h + 1) * HD)
            dk_ref[pl.ds(k0, block), hs] = (state[2 * h] * score_scale).astype(jnp.bfloat16)
            dv_ref[pl.ds(k0, block), hs] = state[2 * h + 1].astype(jnp.bfloat16)
        return carry_none

    lax.fori_loop(0, count, key_loop, 0)
    dqt_ref[...] = (dqt[...] * score_scale).astype(jnp.bfloat16)


def vmem_specs(count):
    return [pl.BlockSpec(memory_space=pltpu.SMEM)] + [
        pl.BlockSpec(memory_space=pltpu.VMEM) for _ in range(count)
    ]


def attend(queries_t, key_all, values_t, segments, slopes):
    rows, cols = key_all.shape
    heads = cols // HD
    block = min(BLOCK, rows)
    vm = pl.BlockSpec(memory_space=pltpu.VMEM)
    return pl.pallas_call(
        functools.partial(attend_kernel, heads, block),
        out_shape=(
            jax.ShapeDtypeStruct((cols, rows), jnp.float32),
            jax.ShapeDtypeStruct((heads, 1, rows), jnp.float32),
        ),
        in_specs=vmem_specs(5),
        out_specs=(vm, vm),
        scratch_shapes=[
            pltpu.VMEM((heads, rows, HD), jnp.bfloat16),
            pltpu.VMEM((block, block), jnp.float32),
        ],
        compiler_params=pltpu.CompilerParams(vmem_limit_bytes=48 * 2**20),
        cost_estimate=pl.CostEstimate(
            flops=40_000_000_000, bytes_accessed=8_000_000, transcendentals=0
        ),
    )(slopes * LOG2E, queries_t, key_all, values_t, segments[None, :], segments[:, None])


def attend_back(queries, queries_t, keys, values, segments, slopes, attended_t, log_sums, grad_out):
    rows, cols = keys.shape
    heads = cols // HD
    block = min(BLOCK, rows)
    vm = pl.BlockSpec(memory_space=pltpu.VMEM)
    per_head = pltpu.VMEM((heads, rows, HD), jnp.bfloat16)
    return pl.pallas_call(
        functools.partial(attend_back_kernel, heads, block),
        out_shape=(
            jax.ShapeDtypeStruct((cols, rows), jnp.bfloat16),
            jax.ShapeDtypeStruct((rows, cols), jnp.bfloat16),
            jax.ShapeDtypeStruct((rows, cols), jnp.bfloat16),
        ),
        in_specs=vmem_specs(11),
        out_specs=(vm, vm, vm),
        scratch_shapes=[
            per_head,
            per_head,
            per_head,
            per_head,
            pltpu.VMEM((heads, 1, rows), jnp.float32),
            pltpu.VMEM((cols, rows), jnp.float32),
            pltpu.VMEM((block, block), jnp.float32),
        ],
        compiler_params=pltpu.CompilerParams(vmem_limit_bytes=48 * 2**20),
        cost_estimate=pl.CostEstimate(
            flops=80_000_000_000, bytes_accessed=16_000_000, transcendentals=0
        ),
    )(
        slopes * LOG2E,
        queries,
        queries_t,
        keys,
        keys.T,
        values,
        grad_out,
        grad_out.T,
        attended_t,
        log_sums,
        segments[None, :],
        segments[:, None],
    )


def pad_lanes(values):
    return jnp.pad(values, ((0, 0), (0, -values.shape[1] % 128)))


def swap_pairs(count, unit, step):
    return [(j, (((j // unit) ^ step) * unit) + j % unit) for j in range(count)]


def place_at(buffer, part, index):
    return lax.dynamic_update_slice_in_dim(buffer, part[None], index, 0)


def gather_level(values, axis, unit):
    count = lax.axis_size(axis)
    group = lax.axis_index(axis) // unit
    buffer = place_at(jnp.zeros((count // unit,) + values.shape, values.dtype), values, group)
    for step in range(1, count // unit):
        part = lax.ppermute(values, axis, swap_pairs(count, unit, step))
        buffer = place_at(buffer, part, group ^ step)
    return buffer


def gather_tensor(values):
    buffer = gather_level(values, "tensor", 1)
    return buffer.reshape((-1,) + values.shape[1:])


def gather_dp(values):
    count = lax.axis_size("dp")
    core = lax.axis_index("dp") % 2
    mine = gather_level(values, "dp", 2)
    other = lax.ppermute(mine, "dp", [(j, j ^ 1) for j in range(count)])
    first = jnp.where(core == 0, mine, other)
    second = jnp.where(core == 0, other, mine)
    return jnp.stack([first, second], axis=1).reshape((-1,) + values.shape[1:])


def pick(values, index):
    return lax.dynamic_index_in_dim(values, index, 0, keepdims=False)


def reduce_level(values, axis, unit):
    count = lax.axis_size(axis)
    group = lax.axis_index(axis) // unit
    total = pick(values, group).astype(jnp.float32)
    for step in range(1, count // unit):
        part = lax.ppermute(pick(values, group ^ step), axis, swap_pairs(count, unit, step))
        total = total + part.astype(jnp.float32)
    return total


def reduce_tensor(values):
    parts = lax.axis_size("tensor")
    return reduce_level(values.reshape((parts, -1) + values.shape[1:]), "tensor", 1)


def reduce_dp(values):
    count = lax.axis_size("dp")
    core = lax.axis_index("dp") % 2
    split = values.reshape((count // 2, 2, values.shape[0] // count) + values.shape[1:])
    keep = lax.dynamic_index_in_dim(split, core, 1, keepdims=False)
    send = lax.dynamic_index_in_dim(split, 1 - core, 1, keepdims=False)
    came = lax.ppermute(send, "dp", [(j, j ^ 1) for j in range(count)])
    both = keep.astype(jnp.float32) + came.astype(jnp.float32)
    return reduce_level(both.astype(values.dtype), "dp", 2)


def body(
    hidden_in,
    ln1_gain,
    ln1_bias,
    qkv_weight,
    qv_bias,
    out_weight,
    out_bias,
    ln2_gain,
    ln2_bias,
    fc_weight,
    fc_bias,
    proj_weight,
    proj_bias,
    segment_ids,
    out_grad,
):
    width = hidden_in.shape[1]
    shard_pos = lax.axis_index("tensor")
    small = (ln1_gain, ln1_bias, qv_bias, out_bias, ln2_gain, ln2_bias, fc_bias, proj_bias)
    packed = gather_dp(gather_tensor(pad_lanes(jnp.concatenate(small)[None, :]))).astype(
        jnp.float32
    )
    device_count = packed.shape[0]
    vectors = []
    place = 0
    for vector in small:
        size = vector.shape[0]
        vectors.append(packed[:, place : place + size].reshape(device_count * size))
        place += size
    gain_one, shift_one, qv_full, out_shift, gain_two, shift_two, fc_full, proj_shift = vectors
    qkv_local, out_local, fc_local, proj_local = (
        lax.all_gather(qkv_weight, "dp", axis=0, tiled=True),
        gather_dp(out_weight),
        gather_dp(fc_weight),
        gather_dp(proj_weight),
    )
    head_cols = qkv_local.shape[2]
    heads_here = head_cols // HD
    ff_cols = fc_local.shape[1]
    ff_total = fc_full.shape[0]
    slopes_all = 2.0 ** (-8.0 * jnp.arange(1, HEADS + 1, dtype=jnp.float32) / HEADS)
    slopes = lax.dynamic_slice_in_dim(slopes_all, shard_pos * heads_here, heads_here)
    q_shift = lax.dynamic_slice_in_dim(qv_full, shard_pos * head_cols, head_cols)
    v_shift = lax.dynamic_slice_in_dim(qv_full, width + shard_pos * head_cols, head_cols)
    source = hidden_in.astype(jnp.float32)
    normed_one = layer_norm(source, gain_one, shift_one)
    group_one = lax.all_gather(normed_one.astype(jnp.bfloat16), "tensor", axis=0, tiled=True)
    group_rows = group_one.shape[0]
    mixed = jnp.einsum("td,dcn->tcn", group_one, qkv_local, preferred_element_type=jnp.float32)
    queries = (mixed[:, 0] + q_shift).astype(jnp.bfloat16)
    keys_here = mixed[:, 1].astype(jnp.bfloat16)
    values_here = (mixed[:, 2] + v_shift).astype(jnp.bfloat16)
    queries_t = queries.T
    attended_t, log_sums = attend(queries_t, keys_here, values_here.T, segment_ids, slopes)
    context = attended_t.astype(jnp.bfloat16).T
    branch_one = lax.psum_scatter(
        contract_cols(context, out_local).astype(jnp.bfloat16),
        "tensor",
        scatter_dimension=0,
        tiled=True,
    ).astype(jnp.float32)
    middle = source + branch_one + out_shift
    normed_two = layer_norm(middle, gain_two, shift_two)
    low_two = normed_two.astype(jnp.bfloat16)
    group_two = lax.all_gather(low_two, "tensor", axis=0, tiled=True)
    fc_shift = lax.dynamic_slice_in_dim(fc_full, shard_pos * ff_cols, ff_cols)
    pre_act = jnp.dot(group_two, fc_local, preferred_element_type=jnp.float32) + fc_shift
    hidden_act = gelu_tanh(pre_act).astype(jnp.bfloat16)
    branch_two = (
        reduce_tensor(contract_cols(hidden_act, proj_local).astype(jnp.bfloat16)) + proj_shift
    )
    result = middle + branch_two
    group_top = gather_tensor(out_grad)
    grad_hidden = jnp.dot(group_top, proj_local, preferred_element_type=jnp.float32)
    grad_proj_local = contract_rows(group_top, hidden_act)
    _, gelu_back = jax.vjp(gelu_tanh, pre_act)
    low_pre = gelu_back(grad_hidden)[0].astype(jnp.bfloat16)
    grad_fc_vec = lax.dynamic_update_slice_in_dim(
        jnp.zeros((ff_total,), jnp.float32),
        jnp.sum(low_pre.astype(jnp.float32), axis=0),
        shard_pos * ff_cols,
        0,
    )
    grad_fc_local = contract_rows(group_two, low_pre)
    grad_normed_two = lax.psum_scatter(
        contract_cols(low_pre, fc_local).astype(jnp.bfloat16),
        "tensor",
        scatter_dimension=0,
        tiled=True,
    ).astype(jnp.float32)
    grad_top = out_grad.astype(jnp.float32)
    grad_proj_vec = jnp.sum(grad_top, axis=0)
    _, norm_two_back = jax.vjp(layer_norm, middle, gain_two, shift_two)
    grad_middle_norm, grad_gain_two, grad_shift_two = norm_two_back(grad_normed_two)
    grad_middle = grad_top + grad_middle_norm
    low_mid = grad_middle.astype(jnp.bfloat16)
    grad_out_vec = jnp.sum(low_mid.astype(jnp.float32), axis=0)
    group_mid = lax.all_gather(low_mid, "tensor", axis=0, tiled=True)
    grad_context = jnp.dot(group_mid, out_local, preferred_element_type=jnp.float32)
    grad_out_local = contract_rows(group_mid, context)
    low_context = grad_context.astype(jnp.bfloat16)
    grad_query_t, grad_key, grad_value = attend_back(
        queries,
        queries_t,
        keys_here,
        values_here,
        segment_ids,
        slopes,
        attended_t,
        log_sums,
        low_context,
    )
    stacked = jnp.stack([grad_query_t.T, grad_key, grad_value], axis=1)
    grad_qkv_local = jnp.einsum(
        "td,tcn->dcn", group_one, stacked, preferred_element_type=jnp.float32
    )
    column_sums = jnp.sum(stacked.astype(jnp.float32), axis=0)
    grad_qv_vec = jnp.zeros((2 * width,), jnp.float32)
    grad_qv_vec = lax.dynamic_update_slice_in_dim(
        grad_qv_vec, column_sums[0], shard_pos * head_cols, 0
    )
    grad_qv_vec = lax.dynamic_update_slice_in_dim(
        grad_qv_vec, column_sums[2], width + shard_pos * head_cols, 0
    )
    grad_normed_one = lax.psum_scatter(
        jnp.einsum("tcn,dcn->td", stacked, qkv_local, preferred_element_type=jnp.float32).astype(
            jnp.bfloat16
        ),
        "tensor",
        scatter_dimension=0,
        tiled=True,
    ).astype(jnp.float32)
    _, norm_one_back = jax.vjp(layer_norm, source, gain_one, shift_one)
    grad_source_norm, grad_gain_one, grad_shift_one = norm_one_back(grad_normed_one)
    grad_input = grad_middle + grad_source_norm
    grad_qkv, grad_out_w, grad_fc_w, grad_proj_w = (
        reduce_dp(grad_qkv_local.astype(jnp.bfloat16)),
        reduce_dp(grad_out_local.astype(jnp.bfloat16)),
        reduce_dp(grad_fc_local.astype(jnp.bfloat16)),
        reduce_dp(grad_proj_local.astype(jnp.bfloat16)),
    )
    grads = (
        grad_gain_one,
        grad_shift_one,
        grad_qv_vec,
        grad_out_vec,
        grad_gain_two,
        grad_shift_two,
        grad_fc_vec,
        grad_proj_vec,
    )
    table = pad_lanes(jnp.concatenate([vec.reshape(device_count, -1) for vec in grads], axis=1))
    dp_count = lax.axis_size("dp")
    by_tensor = jnp.swapaxes(table.reshape(dp_count, -1, table.shape[1]), 0, 1)
    summed = reduce_dp(reduce_level(by_tensor, "tensor", 1)).reshape(-1)
    own = []
    place = 0
    for vector in small:
        size = vector.shape[0]
        own.append(summed[place : place + size])
        place += size
    g_gain_one, g_shift_one, g_qv, g_out_b, g_gain_two, g_shift_two, g_fc_b, g_proj_b = own
    return (
        result.astype(jnp.bfloat16),
        grad_input.astype(jnp.bfloat16),
        g_gain_one,
        g_shift_one,
        grad_qkv,
        g_qv,
        grad_out_w,
        g_out_b,
        g_gain_two,
        g_shift_two,
        grad_fc_w,
        g_fc_b,
        grad_proj_w,
        g_proj_b,
    )


def solution(mesh):
    in_specs = (
        P(("dp", "tensor"), None),
        P(("dp", "tensor")),
        P(("dp", "tensor")),
        P("dp", None, "tensor"),
        P(("dp", "tensor")),
        P("dp", "tensor"),
        P(("dp", "tensor")),
        P(("dp", "tensor")),
        P(("dp", "tensor")),
        P("dp", "tensor"),
        P(("dp", "tensor")),
        P("dp", "tensor"),
        P(("dp", "tensor")),
        P("dp"),
        P(("dp", "tensor"), None),
    )
    out_specs = (
        P(("dp", "tensor"), None),
        P(("dp", "tensor"), None),
        P(("dp", "tensor")),
        P(("dp", "tensor")),
        P("dp", None, "tensor"),
        P(("dp", "tensor")),
        P("dp", "tensor"),
        P(("dp", "tensor")),
        P(("dp", "tensor")),
        P(("dp", "tensor")),
        P("dp", "tensor"),
        P(("dp", "tensor")),
        P("dp", "tensor"),
        P(("dp", "tensor")),
    )
    return jax.shard_map(body, mesh=mesh, in_specs=in_specs, out_specs=out_specs, check_vma=False)
```
